512 devices in a mesh: dp: 32 (over y, x), tensor: 16 (over z, core).
Axes of the slice: x: 4, y: 8, z: 8, core: 2. Of those that a mesh axis runs over, the one named last changes fastest.
Arguments:
- queries: bfloat16 [2, 768, 5, 8192], P(None, 'dp', None, 'tensor'), may hold values from -400 to 400
- kv_cache: bfloat16 [2, 131072, 1024], P(None, ('dp', 'tensor')), may hold values from -6 to 6
- new_kv: bfloat16 [2, 2, 768, 5, 1024], P(None, None, 'dp', None, 'tensor'), may hold values from -6 to 6
- lengths: int32 [32, 24], P('dp'), may hold values from 1 to 341, 4096 in all within a row
- accepted: int32 [2, 768], replicated, may hold values from 0 to 4
- dest: int32 [768], replicated, may hold values from 0 to 767, as said below
Outputs:
- attended: bfloat16 [2, 768, 5, 8192], P(None, 'dp', None, 'tensor')
The draws below stay inside these ranges and needn't reach their ends.
Inputs may be any that keep to these rules, and one draw needn't show every extreme that they name: `dest`: every slot is named by one row; the rows of one replica name at most 2 slots of any one group, and exactly 2 of each group they name. Each group's lengths sum to 4096.
All inputs are finite; a program needn't handle non-finite values.
Results may differ from the reference program's by a relative error of at most 0.002.
Values may be sent and summed in bfloat16 or wider, within the bound.
No kernel may reach another device: no remote copies, remote signals or barrier semaphores. Data moves between devices by JAX's collectives and lax.ppermute only.
A program may use at most 128 MiB of HBM per device.

```python
import math
import jax
import jax.numpy as jnp
import numpy as np
from jax import lax

HQ = 64
KVH = 8
HD = 128
CH = 5
STEPS = 2
RD = 24
GROUPS = 32
ROWS = 768
CAP = 2
LSUM = 4096
LMAX = 341


def draw_queries(key, part):
    key = jax.random.fold_in(key, 5)
    first = jax.random.fold_in(key, 0)
    base = jax.random.normal(first, (STEPS, ROWS, CH, HQ, HD), jnp.float32)
    base = jnp.clip(base, -6.0, 6.0)
    return base.reshape(STEPS, ROWS, CH, HQ * HD).astype(jnp.bfloat16)


def draw_dest(key, part):
    key = jax.random.fold_in(key, 11)
    first, second, third = jax.random.split(key, 3)
    per_source = RD // CAP
    offsets_all = jnp.arange(GROUPS, dtype=jnp.int32)
    special = (offsets_all == 1) | (offsets_all == GROUPS - 1) | (offsets_all == GROUPS // 2)
    shuffled = jax.random.permutation(first, GROUPS).astype(jnp.int32)
    score = jnp.where(special, offsets_all, GROUPS + shuffled)
    shifts = jnp.argsort(score).astype(jnp.int32)[:per_source]
    source_perm = jax.vmap(lambda kk: jax.random.permutation(kk, RD))(jax.random.split(second, GROUPS))
    which = source_perm // CAP
    within = source_perm % CAP
    sources = jnp.arange(GROUPS)[:, None]
    target = (sources + shifts[which]) % GROUPS
    group_perm = jax.vmap(lambda kk: jax.random.permutation(kk, RD))(jax.random.split(third, GROUPS))
    slots = group_perm[target, which * CAP + within]
    return (target * RD + slots).reshape(GROUPS * RD).astype(jnp.int32)


def plant(entries, stream_key, low, largest):
    spot = [jax.random.randint(jax.random.fold_in(stream_key, axis), (), 0, length) for axis, length in enumerate(entries.shape)]
    longest = entries.shape.index(max(entries.shape))
    neighbour = spot[:longest] + [(spot[longest] + 1) % entries.shape[longest]] + spot[longest + 1:]
    return entries.at[tuple(spot)].set(low).at[tuple(neighbour)].set(largest)


def level_of(stream_key, extent, cuts, low, largest):
    level = 1.0
    for axis_at, parts in cuts:
        draws = jax.random.uniform(jax.random.fold_in(jax.random.fold_in(stream_key, 6), axis_at), (parts,), jnp.float32, low / len(cuts), largest / len(cuts))
        level = level * jnp.repeat(jnp.exp(draws), extent[axis_at] // parts).reshape((-1,) + (1,) * (len(extent) - 1 - axis_at))
    return level


def profile(amount, total, bound, skew):
    weights = [(1 << 20) // math.isqrt(grade ** skew) + 1 for grade in range(2, amount + 1)]
    surplus, counts = total - bound - (amount - 1), [1] * (amount - 1)
    while surplus > 0:
        movable = [i for i in range(amount - 1) if counts[i] < bound]
        mass, left = sum([weights[i] for i in movable]), surplus
        for i in movable:
            addition = min(bound - counts[i], max(1, left * weights[i] // mass), surplus)
            counts[i] = counts[i] + addition
            surplus = surplus - addition
    return np.array([bound] + counts)


def uneven(own_key, count, total, most, skew):
    if count == 2:
        one = jax.random.randint(own_key, (), max(1, total - most), min(most, total - 1) + 1)
        return jnp.stack([one, total - one])
    sizes = jnp.asarray(profile(count, total, most, skew), jnp.int32)
    pairs = (count - 1) // 2
    donor, taker = sizes[1:1 + 2 * pairs:2], sizes[2:2 + 2 * pairs:2]
    margin = jnp.minimum(donor - 1, most - taker)
    moved = jax.random.randint(jax.random.fold_in(own_key, 1), (pairs,), 0, 1 << 20) % (margin + 1)
    sizes = sizes.at[1:1 + 2 * pairs:2].set(donor - moved).at[2:2 + 2 * pairs:2].set(taker + moved)
    return sizes[jax.random.permutation(jax.random.fold_in(own_key, 2), count)]


def noise(rng, dims, scale, bound, shards=(), kind=jnp.bfloat16):
    array = jax.random.normal(rng, dims, jnp.float32) * scale
    if len(shards) > 0:
        array = level_of(rng, dims, shards, -0.22, 0.18) * array
    return jnp.clip(array, min=-bound, max=bound).astype(kind)


def setup_inputs(seed: int = 0) -> dict:
    key_of = jax.random.split(jax.random.key(seed), 7)
    return {
        "queries": draw_queries(jax.random.fold_in(key_of[6], 71), 0),
        "kv_cache": noise(key_of[1], (2, GROUPS * LSUM, KVH * HD), 1.0, 6.0, ((1, 512),)),
        "new_kv": noise(key_of[2], (2, STEPS, ROWS, CH, KVH * HD), 1.0, 6.0, ((2, 32), (4, 16))),
        "lengths": jax.vmap(lambda own: uneven(own, RD, LSUM, LMAX, 2))(jax.random.split(key_of[3], GROUPS)).reshape((GROUPS, RD)).astype(jnp.int32),
        "accepted": plant(jax.random.randint(key_of[4], (STEPS, ROWS), 0, CH), jax.random.fold_in(key_of[4], 1), 0, CH - 1).astype(jnp.int32),
        "dest": draw_dest(jax.random.fold_in(key_of[6], 71), 0),
    }


def reference(queries, kv_cache, new_kv, lengths, accepted, dest):
    scale_factor = HD ** -0.5
    repeat = HQ // KVH
    group_of = dest // RD
    slot_of = dest % RD
    starts = jnp.cumsum(lengths, axis=1) - lengths
    offsets = (group_of * LSUM + starts[group_of, slot_of]).astype(jnp.int32)
    row_lens = lengths[group_of, slot_of]
    padded = jnp.pad(kv_cache, ((0, 0), (0, LMAX), (0, 0)))
    step_q = jnp.arange(STEPS * CH) // CH
    pos_q = jnp.arange(STEPS * CH) % CH

    def one_row(row):
        window = lax.dynamic_slice_in_dim(padded, offsets[row], LMAX, 1).astype(jnp.float32)
        window = window.reshape(2, LMAX, KVH, HD)
        query = queries[:, row].astype(jnp.float32).reshape(STEPS * CH, KVH, repeat, HD)
        stretch = new_kv[:, :, row].astype(jnp.float32).reshape(2, STEPS * CH, KVH, HD)
        cache_scores = jnp.einsum("qgrd,pgd->qgrp", query, window[0], precision=lax.Precision.HIGHEST) * scale_factor
        cache_valid = jnp.arange(LMAX) < row_lens[row]
        stretch_scores = jnp.einsum("qgrd,pgd->qgrp", query, stretch[0], precision=lax.Precision.HIGHEST) * scale_factor
        taken = accepted[:, row]
        same = (step_q[None, :] == step_q[:, None]) & (pos_q[None, :] <= pos_q[:, None])
        before = (step_q[None, :] < step_q[:, None]) & (pos_q[None, :] <= taken[step_q][None, :])
        stretch_valid = same | before
        scores = jnp.concatenate([cache_scores, stretch_scores], axis=-1)
        valid = jnp.concatenate([jnp.broadcast_to(cache_valid[None, :], (STEPS * CH, LMAX)), stretch_valid], axis=-1)
        valid = valid[:, None, None, :]
        scores = jnp.where(valid, scores, -1e30)
        top = jnp.max(scores, axis=-1, keepdims=True)
        weights = jnp.where(valid, jnp.exp(scores - top), 0.0)
        total = jnp.sum(weights, axis=-1)
        values = jnp.concatenate([window[1], stretch[1]], axis=0)
        summed = jnp.einsum("qgrp,pgd->qgrd", weights, values, precision=lax.Precision.HIGHEST)
        result = (summed / total[..., None]).reshape(STEPS, CH, HQ * HD)
        keep = jnp.arange(CH)[None, :] <= taken[:, None]
        return jnp.where(keep[:, :, None], result, 0.0)

    every = lax.map(one_row, jnp.arange(ROWS))
    return jnp.transpose(every, (1, 0, 2, 3)).astype(jnp.bfloat16)
```

```python
import jax
import jax.numpy as jnp
from jax import lax
from jax.experimental import pallas as pl
from jax.experimental.pallas import tpu as pltpu
from jax.sharding import PartitionSpec as P

HQ = 64
KVH = 8
HD = 128
CH = 5
STEPS = 2
RD = 24
SPAN = 256
WIN = 384
TOK = STEPS * CH
PER = 4
QR = PER * TOK
SCALE = HD**-0.5
VMEM = pltpu.MemorySpace.VMEM
SMEM = pltpu.MemorySpace.SMEM
LIMIT = 48 * 1024 * 1024


def split_cache(z, kv):
    def kernel(z_ref, kv_ref, own_ref, right_ref, left_ref, sems):
        me = z_ref[0]
        copies = []

        def send(side, dist, dst):
            col = pl.multiple_of(lax.rem(me + dist, KVH) * HD, HD)
            sem = sems.at[len(copies)]
            copies.append(
                pltpu.make_async_copy(kv_ref.at[side, :, pl.ds(col, HD)], dst, sem)
            )

        for side in range(2):
            for dist in range(1, 4):
                send(side, dist, right_ref.at[2 * (dist - 1) + side])
                send(side, KVH - dist, left_ref.at[2 * (dist - 1) + side])
            send(side, 0, own_ref.at[side])
        send(0, 4, right_ref.at[6])
        send(1, 4, left_ref.at[6])
        for copy in copies:
            copy.start()
        for copy in copies:
            copy.wait()

    return pl.pallas_call(
        kernel,
        out_shape=(
            jax.ShapeDtypeStruct((2, SPAN, HD), kv.dtype),
            jax.ShapeDtypeStruct((7, SPAN, HD), kv.dtype),
            jax.ShapeDtypeStruct((7, SPAN, HD), kv.dtype),
        ),
        in_specs=[pl.BlockSpec(memory_space=SMEM), pl.BlockSpec(memory_space=pl.ANY)],
        out_specs=[pl.BlockSpec(memory_space=pl.ANY)] * 3,
        scratch_shapes=[pltpu.SemaphoreType.DMA((16,))],
        cost_estimate=pl.CostEstimate(flops=0, bytes_accessed=2 << 20, transcendentals=0),
        name="split_cache",
    )(z, kv)


def pack_rows(pos, queries, new_kv):
    def kernel(pos_ref, q_ref, n_ref, out_ref, qs, ns):
        for j in range(RD):
            at = pos_ref[j]
            for s in range(STEPS):
                q = q_ref[s, j].astype(jnp.float32)
                for h in range(PER):
                    row = h * TOK + s * CH
                    qs[at, row : row + CH, :] = q[:, h * HD : (h + 1) * HD]
                n = jnp.concatenate([n_ref[0, s, j], n_ref[1, s, j]], axis=-1)
                ns[at, s * CH : (s + 1) * CH, :] = n.astype(jnp.float32)
        for g in range(32):
            block = [qs[2 * g], qs[2 * g + 1], ns[2 * g], ns[2 * g + 1]]
            out_ref[g] = jnp.concatenate(block, axis=0).astype(jnp.bfloat16)

    return pl.pallas_call(
        kernel,
        out_shape=jax.ShapeDtypeStruct((32, 2 * (QR + TOK), HD), jnp.bfloat16),
        in_specs=[
            pl.BlockSpec(memory_space=SMEM),
            pl.BlockSpec(memory_space=VMEM),
            pl.BlockSpec(memory_space=VMEM),
        ],
        out_specs=pl.BlockSpec(memory_space=VMEM),
        scratch_shapes=[
            pltpu.VMEM((64, QR, HD), jnp.float32),
            pltpu.VMEM((64, TOK, HD), jnp.float32),
        ],
        compiler_params=pltpu.CompilerParams(vmem_limit_bytes=LIMIT),
        cost_estimate=pl.CostEstimate(flops=0, bytes_accessed=2 << 20, transcendentals=0),
        name="pack_rows",
    )(pos, queries, new_kv)


def attend(info, received, new_sib, pieces, sib):
    n_pieces = len(pieces)
    layout = []
    for i, dist in enumerate((0, -1, 1, -2, 2, -3, 3)):
        layout += [(i, 0, 0, dist), (i, 1, 1, dist)]
    layout += [(7, 0, 0, 4), (8, 0, 1, 4)]

    def kernel(info_ref, recv_ref, ns_ref, *refs):
        piece_refs = refs[:n_pieces]
        sib_ref, out_ref, kbuf, vbuf, qs, kn, vn, sems = refs[n_pieces:]
        z, core = info_ref[5, 0], info_ref[5, 1]
        copies = []
        for unit, (i, u, side, dist) in enumerate(layout):
            src_z = lax.rem(z + dist + KVH, KVH)
            for other in range(2):
                owner = src_z * 2 + (core if other == 0 else 1 - core)
                rows = pl.ds(pl.multiple_of(owner * SPAN, SPAN), SPAN)
                src = piece_refs[i].at[u] if other == 0 else sib_ref.at[unit]
                dst = (kbuf, vbuf)[side].at[rows]
                copies.append(pltpu.make_async_copy(src, dst, sems.at[len(copies)]))
        for copy in copies:
            copy.start()
        kbuf[KVH * 2 * SPAN :, :] = jnp.zeros((WIN, HD), jnp.bfloat16)
        vbuf[KVH * 2 * SPAN :, :] = jnp.zeros((WIN, HD), jnp.bfloat16)
        low_half = lax.broadcasted_iota(jnp.int32, (TOK, HD), 1) < HD // 2
        fill = jnp.zeros((16 - TOK, HD), jnp.float32)
        for j in range(RD):
            at = info_ref[0, j]
            g, second = at // 2, lax.rem(at, 2) == 1
            block = recv_ref[g].astype(jnp.float32)
            other = ns_ref[g].astype(jnp.float32)
            qs[j] = jnp.where(second, block[QR : 2 * QR], block[:QR]).astype(jnp.bfloat16)
            base = 2 * QR
            mine = jnp.where(second, block[base + TOK :], block[base : base + TOK])
            theirs = jnp.where(second, other[TOK:], other[:TOK])
            low = jnp.where(core == 0, mine, theirs)
            high = jnp.where(core == 0, theirs, mine)
            key = jnp.where(low_half, low, pltpu.roll(high, HD // 2, 1))
            value = jnp.where(low_half, pltpu.roll(low, HD // 2, 1), high)
            kn[j] = jnp.concatenate([key, fill], axis=0).astype(jnp.bfloat16)
            vn[j] = jnp.concatenate([value, fill], axis=0).astype(jnp.bfloat16)
        col = lax.broadcasted_iota(jnp.int32, (QR, WIN), 1)
        ncol = lax.broadcasted_iota(jnp.int32, (QR, 16), 1)
        nrow = lax.rem(lax.broadcasted_iota(jnp.int32, (QR, 16), 0), TOK)
        step_k, step_q = ncol // CH, nrow // CH
        pos_k, pos_q = lax.rem(ncol, CH), lax.rem(nrow, CH)
        need = jnp.where((step_k == step_q) & (pos_k <= pos_q), -1, 100)
        need = jnp.where(step_k < step_q, pos_k, need)
        need = jnp.where(ncol < TOK, need, 100)
        trow = lax.rem(lax.broadcasted_iota(jnp.int32, (QR, HD), 0), TOK)
        tstep, tpos = trow // CH, lax.rem(trow, CH)
        for copy in copies:
            copy.wait()

        group = 6

        def some(it, carry):
            js = [it * group + i for i in range(group)]
            scores, values = [], []
            for j in js:
                start, length = info_ref[1, j], info_ref[2, j]
                base = pl.multiple_of((start // 16) * 16, 16)
                off = start - base
                keys = jnp.concatenate([kbuf[pl.ds(base, WIN), :], kn[j]], axis=0)
                sc = lax.dot_general(
                    qs[j], keys, (((1,), (1,)), ((), ())), preferred_element_type=jnp.float32
                )
                cached = jnp.where(
                    (col >= off) & (col < off + length), sc[:, :WIN] * SCALE, -1e30
                )
                fresh = jnp.where(need <= info_ref[3, j], sc[:, WIN:] * SCALE, -1e30)
                scores.append((cached, fresh))
            weights = []
            for cached, fresh in scores:
                top = jnp.maximum(
                    jnp.max(cached, axis=1, keepdims=True), jnp.max(fresh, axis=1, keepdims=True)
                )
                wc, wf = jnp.exp(cached - top), jnp.exp(fresh - top)
                total = jnp.sum(wc, axis=1, keepdims=True) + jnp.sum(wf, axis=1, keepdims=True)
                weights.append((jnp.concatenate([wc, wf], axis=1), total))
            for j, (w, total) in zip(js, weights):
                base = pl.multiple_of((info_ref[1, j] // 16) * 16, 16)
                vals = jnp.concatenate([vbuf[pl.ds(base, WIN), :], vn[j]], axis=0)
                high = w.astype(jnp.bfloat16)
                low = (w - high.astype(jnp.float32)).astype(jnp.bfloat16)
                dims = (((1,), (0,)), ((), ()))
                acc = lax.dot_general(high, vals, dims, preferred_element_type=jnp.float32)
                acc += lax.dot_general(low, vals, dims, preferred_element_type=jnp.float32)
                limit = jnp.where(tstep == 0, info_ref[3, j], info_ref[4, j])
                out = jnp.where(tpos <= limit, acc / total, 0.0)
                out_ref[info_ref[0, j]] = out.astype(jnp.bfloat16)
            return carry

        lax.fori_loop(0, RD // group, some, 0)

    return pl.pallas_call(
        kernel,
        out_shape=jax.ShapeDtypeStruct((64, QR, HD), jnp.bfloat16),
        in_specs=[
            pl.BlockSpec(memory_space=SMEM),
            pl.BlockSpec(memory_space=VMEM),
            pl.BlockSpec(memory_space=VMEM),
        ]
        + [pl.BlockSpec(memory_space=pl.ANY)] * (n_pieces + 1),
        out_specs=pl.BlockSpec(memory_space=VMEM),
        scratch_shapes=[
            pltpu.VMEM((KVH * 2 * SPAN + WIN, HD), jnp.bfloat16),
            pltpu.VMEM((KVH * 2 * SPAN + WIN, HD), jnp.bfloat16),
            pltpu.VMEM((RD, QR, HD), jnp.bfloat16),
            pltpu.VMEM((RD, 16, HD), jnp.bfloat16),
            pltpu.VMEM((RD, 16, HD), jnp.bfloat16),
            pltpu.SemaphoreType.DMA((32,)),
        ],
        compiler_params=pltpu.CompilerParams(vmem_limit_bytes=LIMIT),
        cost_estimate=pl.CostEstimate(
            flops=24 * 40 * 400 * 128 * 6, bytes_accessed=4 << 20, transcendentals=24 * 40 * 400
        ),
        name="attend",
    )(info, received, new_sib, *pieces, sib)


def unpack_rows(pos, received):
    def kernel(pos_ref, in_ref, out_ref):
        for j in range(RD):
            block = in_ref[pos_ref[j]].astype(jnp.float32)
            for s in range(STEPS):
                heads = [block[h * TOK + s * CH : h * TOK + (s + 1) * CH] for h in range(PER)]
                out_ref[s, j] = jnp.concatenate(heads, axis=1).astype(jnp.bfloat16)

    return pl.pallas_call(
        kernel,
        out_shape=jax.ShapeDtypeStruct((STEPS, RD, CH, PER * HD), jnp.bfloat16),
        in_specs=[pl.BlockSpec(memory_space=SMEM), pl.BlockSpec(memory_space=VMEM)],
        out_specs=pl.BlockSpec(memory_space=VMEM),
        compiler_params=pltpu.CompilerParams(vmem_limit_bytes=LIMIT),
        cost_estimate=pl.CostEstimate(flops=0, bytes_accessed=1 << 20, transcendentals=0),
        name="unpack_rows",
    )(pos, received)


def body(queries, kv_cache, new_kv, lengths, accepted, dest):
    me_dp = lax.axis_index("dp")
    me_ten = lax.axis_index("tensor")
    z, core = me_ten // 2, me_ten % 2
    n_dp = lax.axis_size("dp")

    def along_z(x, k):
        perm = [(t, (t // 2 + k) % KVH * 2 + t % 2) for t in range(16)]
        return lax.ppermute(x, "tensor", perm)

    def sibling(x):
        return lax.ppermute(x, "tensor", [(t, t ^ 1) for t in range(16)])

    own, right, left = split_cache(z.reshape(1).astype(jnp.int32), kv_cache)
    pieces = [own]
    for _ in range(4):
        right, left = along_z(right, 1), along_z(left, -1)
        pieces += [right[:2], left[:2]]
        right, left = right[2:], left[2:]

    group_of = dest // RD
    mine = lax.dynamic_slice_in_dim(group_of, me_dp * RD, RD)
    order = jnp.arange(RD)
    rank = jnp.sum((mine[:, None] == mine[None, :]) & (order[None, :] < order[:, None]), axis=1)
    send_pos = (mine * 2 + rank).astype(jnp.int32)
    here = (group_of == me_dp).reshape(n_dp, RD)
    before = jnp.sum(here[:, None, :] & (order[None, :] < order[:, None]), axis=2)
    place = (jnp.arange(n_dp)[:, None] * 2 + before).reshape(-1)
    hit = dest[None, :] == (me_dp * RD + order)[:, None]
    recv_pos = jnp.sum(jnp.where(hit, place[None, :], 0), axis=1)
    taken = jnp.sum(jnp.where(hit[None], accepted[:, None, :], 0), axis=2)
    length = lengths[0]
    start = jnp.sum(jnp.where(order[None, :] < order[:, None], length[None, :], 0), axis=1)
    ident = jnp.where(order == 0, z, jnp.where(order == 1, core, 0))
    info = jnp.stack([recv_pos, start, length, taken[0], taken[1], ident]).astype(jnp.int32)

    packed = pack_rows(send_pos, queries, new_kv)
    received = lax.all_to_all(packed, "dp", split_axis=0, concat_axis=0, tiled=True)
    new_sib = sibling(received[:, 2 * QR :])
    sib = sibling(jnp.concatenate(pieces, axis=0))
    outs = attend(info, received, new_sib, pieces, sib)
    back = lax.all_to_all(
        outs.reshape(n_dp, 2 * QR, HD), "dp", split_axis=0, concat_axis=0, tiled=True
    )
    return unpack_rows(send_pos, back.reshape(2 * n_dp, QR, HD))


def solution(mesh):
    return jax.shard_map(
        body,
        mesh=mesh,
        in_specs=(
            P(None, "dp", None, "tensor"),
            P(None, ("dp", "tensor"), None),
            P(None, None, "dp", None, "tensor"),
            P("dp", None),
            P(),
            P(),
        ),
        out_specs=P(None, "dp", None, "tensor"),
        check_vma=False,
    )
```

```python
import jax
import jax.numpy as jnp
from jax import lax
from jax.experimental import pallas as pl
from jax.experimental.pallas import tpu as pltpu
from jax.sharding import PartitionSpec as P

HQ = 64
KVH = 8
HD = 128
CH = 5
STEPS = 2
RD = 24
SPAN = 256
WIN = 384
TOK = STEPS * CH
PER = 4
QR = PER * TOK
SCALE = HD**-0.5
VMEM = pltpu.MemorySpace.VMEM
SMEM = pltpu.MemorySpace.SMEM
LIMIT = 48 * 1024 * 1024


def split_cache(ident, kv):
    def kernel(id_ref, kv_ref, keep_ref, give_ref):
        z, core = id_ref[0], id_ref[1]
        step = 1 - 2 * core

        def cut(side, dist):
            col = pl.multiple_of(lax.rem(z + dist + KVH, KVH) * HD, HD)
            return kv_ref[side, :, pl.ds(col, HD)]

        for dist in range(1, 4):
            for side in range(2):
                keep_ref[2 * (dist - 1) + side] = cut(side, dist * step)
                give_ref[2 * (dist - 1) + side] = cut(side, -dist * step)
        keep_ref[6] = cut(core, 4)
        give_ref[6] = cut(1 - core, 4)
        give_ref[7] = cut(0, 0)
        give_ref[8] = cut(1, 0)

    return pl.pallas_call(
        kernel,
        out_shape=(
            jax.ShapeDtypeStruct((7, SPAN, HD), kv.dtype),
            jax.ShapeDtypeStruct((9, SPAN, HD), kv.dtype),
        ),
        in_specs=[pl.BlockSpec(memory_space=SMEM), pl.BlockSpec(memory_space=VMEM)],
        out_specs=[pl.BlockSpec(memory_space=VMEM)] * 2,
        compiler_params=pltpu.CompilerParams(vmem_limit_bytes=LIMIT),
        cost_estimate=pl.CostEstimate(flops=0, bytes_accessed=2 << 20, transcendentals=0),
        name="split_cache",
    )(ident, kv)


def pack_rows(pos, queries, new_kv):
    def kernel(pos_ref, q_ref, n_ref, out_ref, qs, ns):
        for j in range(RD):
            at = pos_ref[j]
            for s in range(STEPS):
                q = q_ref[s, j].astype(jnp.float32)
                for h in range(PER):
                    row = h * TOK + s * CH
                    qs[at, row : row + CH, :] = q[:, h * HD : (h + 1) * HD]
                n = jnp.concatenate([n_ref[0, s, j], n_ref[1, s, j]], axis=-1)
                ns[at, s * CH : (s + 1) * CH, :] = n.astype(jnp.float32)
        for g in range(32):
            block = [qs[2 * g], qs[2 * g + 1], ns[2 * g], ns[2 * g + 1]]
            out_ref[g] = jnp.concatenate(block, axis=0).astype(jnp.bfloat16)

    return pl.pallas_call(
        kernel,
        out_shape=jax.ShapeDtypeStruct((32, 2 * (QR + TOK), HD), jnp.bfloat16),
        in_specs=[
            pl.BlockSpec(memory_space=SMEM),
            pl.BlockSpec(memory_space=VMEM),
            pl.BlockSpec(memory_space=VMEM),
        ],
        out_specs=pl.BlockSpec(memory_space=VMEM),
        scratch_shapes=[
            pltpu.VMEM((64, QR, HD), jnp.float32),
            pltpu.VMEM((64, TOK, HD), jnp.float32),
        ],
        compiler_params=pltpu.CompilerParams(vmem_limit_bytes=LIMIT),
        cost_estimate=pl.CostEstimate(flops=0, bytes_accessed=2 << 20, transcendentals=0),
        name="pack_rows",
    )(pos, queries, new_kv)


def attend(info, received, new_sib, pieces):
    n_pieces = len(pieces)

    def kernel(info_ref, recv_ref, ns_ref, *refs):
        piece_refs = refs[:n_pieces]
        out_ref, kvbuf, qs, kn, vn, sems = refs[n_pieces:]
        z, core = info_ref[5, 0], info_ref[5, 1]
        step = 1 - 2 * core
        copies = []

        def place(piece, unit, side, src_z, src_core):
            owner = lax.rem(src_z + KVH, KVH) * 2 + src_core
            rows = pl.ds(pl.multiple_of(owner * SPAN, SPAN), SPAN)
            copies.append(
                pltpu.make_async_copy(
                    piece_refs[piece].at[unit], kvbuf.at[side, rows], sems.at[len(copies)]
                )
            )

        for side in range(2):
            place(0, 7 + side, side, z, core)
            place(1, 7 + side, side, z, 1 - core)
            for dist in range(1, 4):
                for half in range(2):
                    unit = 2 * half + side
                    there = core if half == 0 else 1 - core
                    place(1 + dist, unit, side, z - step * dist, there)
                    far, at = (6, 4 * (dist - 1)) if dist < 3 else (7, 0)
                    place(far, at + unit, side, z + step * dist, 1 - there)
        for half in range(2):
            there = core if half == 0 else 1 - core
            place(5, half, core, z + 4, there)
            place(7, 4 + half, 1 - core, z + 4, 1 - there)
        for copy in copies:
            copy.start()
        kvbuf[:, KVH * 2 * SPAN :, :] = jnp.zeros((2, WIN, HD), jnp.bfloat16)
        low_half = lax.broadcasted_iota(jnp.int32, (TOK, HD), 1) < HD // 2
        fill = jnp.zeros((16 - TOK, HD), jnp.float32)
        for j in range(RD):
            at = info_ref[0, j]
            g, second = at // 2, lax.rem(at, 2) == 1
            block = recv_ref[g].astype(jnp.float32)
            other = ns_ref[g].astype(jnp.float32)
            qs[j] = jnp.where(second, block[QR : 2 * QR], block[:QR]).astype(jnp.bfloat16)
            base = 2 * QR
            mine = jnp.where(second, block[base + TOK :], block[base : base + TOK])
            theirs = jnp.where(second, other[TOK:], other[:TOK])
            low = jnp.where(core == 0, mine, theirs)
            high = jnp.where(core == 0, theirs, mine)
            key = jnp.where(low_half, low, pltpu.roll(high, HD // 2, 1))
            value = jnp.where(low_half, pltpu.roll(low, HD // 2, 1), high)
            kn[j] = jnp.concatenate([key, fill], axis=0).astype(jnp.bfloat16)
            vn[j] = jnp.concatenate([value, fill], axis=0).astype(jnp.bfloat16)
        col = lax.broadcasted_iota(jnp.int32, (QR, WIN), 1)
        ncol = lax.broadcasted_iota(jnp.int32, (QR, 16), 1)
        nrow = lax.rem(lax.broadcasted_iota(jnp.int32, (QR, 16), 0), TOK)
        step_k, step_q = ncol // CH, nrow // CH
        pos_k, pos_q = lax.rem(ncol, CH), lax.rem(nrow, CH)
        need = jnp.where((step_k == step_q) & (pos_k <= pos_q), -1, 100)
        need = jnp.where(step_k < step_q, pos_k, need)
        need = jnp.where(ncol < TOK, need, 100)
        trow = lax.rem(lax.broadcasted_iota(jnp.int32, (QR, HD), 0), TOK)
        tstep, tpos = trow // CH, lax.rem(trow, CH)
        for copy in copies:
            copy.wait()

        group = 6

        def some(it, carry):
            js = [it * group + i for i in range(group)]
            scores, values = [], []
            for j in js:
                start, length = info_ref[1, j], info_ref[2, j]
                base = pl.multiple_of((start // 16) * 16, 16)
                off = start - base
                keys = jnp.concatenate([kvbuf[0, pl.ds(base, WIN), :], kn[j]], axis=0)
                sc = lax.dot_general(
                    qs[j], keys, (((1,), (1,)), ((), ())), preferred_element_type=jnp.float32
                )
                cached = jnp.where(
                    (col >= off) & (col < off + length), sc[:, :WIN] * SCALE, -1e30
                )
                fresh = jnp.where(need <= info_ref[3, j], sc[:, WIN:] * SCALE, -1e30)
                scores.append((cached, fresh))
            weights = []
            for cached, fresh in scores:
                top = jnp.maximum(
                    jnp.max(cached, axis=1, keepdims=True), jnp.max(fresh, axis=1, keepdims=True)
                )
                wc, wf = jnp.exp(cached - top), jnp.exp(fresh - top)
                total = jnp.sum(wc, axis=1, keepdims=True) + jnp.sum(wf, axis=1, keepdims=True)
                weights.append((jnp.concatenate([wc, wf], axis=1), total))
            for j, (w, total) in zip(js, weights):
                base = pl.multiple_of((info_ref[1, j] // 16) * 16, 16)
                vals = jnp.concatenate([kvbuf[1, pl.ds(base, WIN), :], vn[j]], axis=0)
                high = w.astype(jnp.bfloat16)
                low = (w - high.astype(jnp.float32)).astype(jnp.bfloat16)
                dims = (((1,), (0,)), ((), ()))
                acc = lax.dot_general(high, vals, dims, preferred_element_type=jnp.float32)
                acc += lax.dot_general(low, vals, dims, preferred_element_type=jnp.float32)
                limit = jnp.where(tstep == 0, info_ref[3, j], info_ref[4, j])
                out = jnp.where(tpos <= limit, acc / total, 0.0)
                out_ref[info_ref[0, j]] = out.astype(jnp.bfloat16)
            return carry

        lax.fori_loop(0, RD // group, some, 0)

    return pl.pallas_call(
        kernel,
        out_shape=jax.ShapeDtypeStruct((64, QR, HD), jnp.bfloat16),
        in_specs=[
            pl.BlockSpec(memory_space=SMEM),
            pl.BlockSpec(memory_space=VMEM),
            pl.BlockSpec(memory_space=VMEM),
        ]
        + [pl.BlockSpec(memory_space=pl.ANY)] * n_pieces,
        out_specs=pl.BlockSpec(memory_space=VMEM),
        scratch_shapes=[
            pltpu.VMEM((2, KVH * 2 * SPAN + WIN, HD), jnp.bfloat16),
            pltpu.VMEM((RD, QR, HD), jnp.bfloat16),
            pltpu.VMEM((RD, 16, HD), jnp.bfloat16),
            pltpu.VMEM((RD, 16, HD), jnp.bfloat16),
            pltpu.SemaphoreType.DMA((32,)),
        ],
        compiler_params=pltpu.CompilerParams(vmem_limit_bytes=LIMIT),
        cost_estimate=pl.CostEstimate(
            flops=24 * 40 * 400 * 128 * 6, bytes_accessed=4 << 20, transcendentals=24 * 40 * 400
        ),
        name="attend",
    )(info, received, new_sib, *pieces)


def unpack_rows(pos, received):
    def kernel(pos_ref, in_ref, out_ref):
        for j in range(RD):
            block = in_ref[pos_ref[j]].astype(jnp.float32)
            for s in range(STEPS):
                heads = [block[h * TOK + s * CH : h * TOK + (s + 1) * CH] for h in range(PER)]
                out_ref[s, j] = jnp.concatenate(heads, axis=1).astype(jnp.bfloat16)

    return pl.pallas_call(
        kernel,
        out_shape=jax.ShapeDtypeStruct((STEPS, RD, CH, PER * HD), jnp.bfloat16),
        in_specs=[pl.BlockSpec(memory_space=SMEM), pl.BlockSpec(memory_space=VMEM)],
        out_specs=pl.BlockSpec(memory_space=VMEM),
        compiler_params=pltpu.CompilerParams(vmem_limit_bytes=LIMIT),
        cost_estimate=pl.CostEstimate(flops=0, bytes_accessed=1 << 20, transcendentals=0),
        name="unpack_rows",
    )(pos, received)


def body(queries, kv_cache, new_kv, lengths, accepted, dest):
    me_dp = lax.axis_index("dp")
    me_ten = lax.axis_index("tensor")
    z, core = me_ten // 2, me_ten % 2
    n_dp = lax.axis_size("dp")

    def along_z(x, k):
        perm = [(t, (t // 2 + (k if t % 2 == 0 else -k)) % KVH * 2 + t % 2) for t in range(16)]
        return lax.ppermute(x, "tensor", perm)

    def sibling(x):
        return lax.ppermute(x, "tensor", [(t, t ^ 1) for t in range(16)])

    keep, give = split_cache(jnp.stack([z, core]).astype(jnp.int32), kv_cache)
    got = sibling(give)
    moved = []
    for k in range(1, 5):
        cut = slice(2 * k - 2, min(2 * k, 7))
        moved.append(along_z(jnp.concatenate([keep[cut], got[cut]], axis=0), k))
    crossed_a = sibling(jnp.concatenate(moved[:2], axis=0))
    crossed_b = sibling(jnp.concatenate(moved[2:], axis=0))
    pieces = [give, got] + moved + [crossed_a, crossed_b]

    group_of = dest // RD
    mine = lax.dynamic_slice_in_dim(group_of, me_dp * RD, RD)
    order = jnp.arange(RD)
    rank = jnp.sum((mine[:, None] == mine[None, :]) & (order[None, :] < order[:, None]), axis=1)
    send_pos = (mine * 2 + rank).astype(jnp.int32)
    here = (group_of == me_dp).reshape(n_dp, RD)
    before = jnp.sum(here[:, None, :] & (order[None, :] < order[:, None]), axis=2)
    place = (jnp.arange(n_dp)[:, None] * 2 + before).reshape(-1)
    hit = dest[None, :] == (me_dp * RD + order)[:, None]
    recv_pos = jnp.sum(jnp.where(hit, place[None, :], 0), axis=1)
    taken = jnp.sum(jnp.where(hit[None], accepted[:, None, :], 0), axis=2)
    length = lengths[0]
    start = jnp.sum(jnp.where(order[None, :] < order[:, None], length[None, :], 0), axis=1)
    ident = jnp.where(order == 0, z, jnp.where(order == 1, core, 0))
    info = jnp.stack([recv_pos, start, length, taken[0], taken[1], ident]).astype(jnp.int32)

    packed = pack_rows(send_pos, queries, new_kv)
    received = lax.all_to_all(packed, "dp", split_axis=0, concat_axis=0, tiled=True)
    new_sib = sibling(received[:, 2 * QR :])
    outs = attend(info, received, new_sib, pieces)
    back = lax.all_to_all(
        outs.reshape(n_dp, 2 * QR, HD), "dp", split_axis=0, concat_axis=0, tiled=True
    )
    return unpack_rows(send_pos, back.reshape(2 * n_dp, QR, HD))


def solution(mesh):
    return jax.shard_map(
        body,
        mesh=mesh,
        in_specs=(
            P(None, "dp", None, "tensor"),
            P(None, ("dp", "tensor"), None),
            P(None, None, "dp", None, "tensor"),
            P("dp", None),
            P(),
            P(),
        ),
        out_specs=P(None, "dp", None, "tensor"),
        check_vma=False,
    )
```

```python
import jax
import jax.numpy as jnp
from jax import lax
from jax.experimental import pallas as pl
from jax.experimental.pallas import tpu as pltpu
from jax.sharding import PartitionSpec as P

HQ = 64
KVH = 8
HD = 128
CH = 5
STEPS = 2
RD = 24
SPAN = 256
WIN = 384
TOK = STEPS * CH
PER = 4
QR = PER * TOK
SCALE = HD**-0.5
VMEM = pltpu.MemorySpace.VMEM
SMEM = pltpu.MemorySpace.SMEM
LIMIT = 48 * 1024 * 1024


def split_cache(ident, kv):
    def kernel(id_ref, kv_ref, keep_ref, give_ref, sems):
        z, core = id_ref[0], id_ref[1]
        step = 1 - 2 * core
        copies = []

        def put(ref, unit, side, dist):
            col = pl.multiple_of(lax.rem(z + dist + KVH, KVH) * HD, HD)
            src = kv_ref.at[side, :, pl.ds(col, HD)]
            dst = ref.at[pl.ds(unit * SPAN, SPAN)]
            copies.append(pltpu.make_async_copy(src, dst, sems.at[len(copies)]))

        for dist in range(1, 4):
            for side in range(2):
                put(give_ref, 2 * (dist - 1) + side, side, -dist * step)
                put(keep_ref, 2 * (dist - 1) + side, side, dist * step)
        put(give_ref, 6, 1 - core, 4)
        put(keep_ref, 6, core, 4)
        put(give_ref, 7, 0, 0)
        put(give_ref, 8, 1, 0)
        for copy in copies:
            copy.start()
        for copy in copies:
            copy.wait()

    return pl.pallas_call(
        kernel,
        out_shape=(
            jax.ShapeDtypeStruct((7 * SPAN, HD), kv.dtype),
            jax.ShapeDtypeStruct((9 * SPAN, HD), kv.dtype),
        ),
        in_specs=[pl.BlockSpec(memory_space=SMEM), pl.BlockSpec(memory_space=pl.ANY)],
        out_specs=[pl.BlockSpec(memory_space=VMEM)] * 2,
        scratch_shapes=[pltpu.SemaphoreType.DMA((16,))],
        compiler_params=pltpu.CompilerParams(vmem_limit_bytes=LIMIT),
        cost_estimate=pl.CostEstimate(flops=0, bytes_accessed=2 << 20, transcendentals=0),
        name="split_cache",
    )(ident, kv)


def join_cores(keep, got):
    sizes = [4, 4, 4, 2]

    def kernel(keep_ref, got_ref, *outs):
        for i, out in enumerate(outs):
            rows = sizes[i] // 2 * SPAN
            out[:rows, :] = keep_ref[2 * i * SPAN : 2 * i * SPAN + rows, :]
            out[rows:, :] = got_ref[2 * i * SPAN : 2 * i * SPAN + rows, :]

    return pl.pallas_call(
        kernel,
        out_shape=[jax.ShapeDtypeStruct((n * SPAN, HD), keep.dtype) for n in sizes],
        in_specs=[pl.BlockSpec(memory_space=VMEM)] * 2,
        out_specs=[pl.BlockSpec(memory_space=VMEM)] * 4,
        compiler_params=pltpu.CompilerParams(vmem_limit_bytes=LIMIT),
        cost_estimate=pl.CostEstimate(flops=0, bytes_accessed=2 << 20, transcendentals=0),
        name="join_cores",
    )(keep, got)


def pack_rows(dest, first, queries, new_kv):
    def kernel(dest_ref, first_ref, q_ref, n_ref, out_ref, pos_ref, seen, qf, nf, qs, ns):
        for g in range(32):
            seen[g] = 0
        for j in range(RD):
            g = dest_ref[first_ref[0] + j] // RD
            pos_ref[j] = 2 * g + seen[g]
            seen[g] = 1
        for s in range(STEPS):
            for c in range(CH):
                row = (s * CH + c) * RD
                q = q_ref[s, c].astype(jnp.float32)
                for h in range(PER):
                    qf[h, row : row + RD, :] = q[:, h * HD : (h + 1) * HD]
                n = [n_ref[side, s, c].astype(jnp.float32) for side in range(2)]
                nf[row : row + RD, :] = jnp.concatenate(n, axis=1)
        for j in range(RD):
            at = pos_ref[j]
            for s in range(STEPS):
                rows = pl.ds(s * CH * RD + j, CH, stride=RD)
                for h in range(PER):
                    row = h * TOK + s * CH
                    qs[at, row : row + CH, :] = qf[h, rows, :]
                ns[at, s * CH : (s + 1) * CH, :] = nf[rows, :]
        for g in range(32):
            block = [qs[2 * g], qs[2 * g + 1], ns[2 * g], ns[2 * g + 1]]
            out_ref[g] = jnp.concatenate(block, axis=0).astype(jnp.bfloat16)

    return pl.pallas_call(
        kernel,
        out_shape=(
            jax.ShapeDtypeStruct((32, 2 * (QR + TOK), HD), jnp.bfloat16),
            jax.ShapeDtypeStruct((RD,), jnp.int32),
        ),
        in_specs=[
            pl.BlockSpec(memory_space=SMEM),
            pl.BlockSpec(memory_space=SMEM),
            pl.BlockSpec(memory_space=VMEM),
            pl.BlockSpec(memory_space=VMEM),
        ],
        out_specs=(pl.BlockSpec(memory_space=VMEM), pl.BlockSpec(memory_space=SMEM)),
        scratch_shapes=[
            pltpu.SMEM((32,), jnp.int32),
            pltpu.VMEM((PER, TOK * RD, HD), jnp.float32),
            pltpu.VMEM((TOK * RD, HD), jnp.float32),
            pltpu.VMEM((64, QR, HD), jnp.float32),
            pltpu.VMEM((64, TOK, HD), jnp.float32),
        ],
        compiler_params=pltpu.CompilerParams(vmem_limit_bytes=LIMIT),
        cost_estimate=pl.CostEstimate(flops=0, bytes_accessed=2 << 20, transcendentals=0),
        name="pack_rows",
    )(dest, first, queries, new_kv)


def pick_rows(info, received):
    def kernel(info_ref, recv_ref, q_ref, n_ref):
        fill = jnp.zeros((16 - TOK, HD), jnp.float32)
        base = 2 * QR
        for j in range(RD):
            at = info_ref[0, j]
            g, second = at // 2, lax.rem(at, 2) == 1
            block = recv_ref[g].astype(jnp.float32)
            q_ref[j] = jnp.where(second, block[QR : 2 * QR], block[:QR]).astype(jnp.bfloat16)
            fresh = jnp.where(second, block[base + TOK :], block[base : base + TOK])
            n_ref[16 * j : 16 * j + 16, :] = jnp.concatenate([fresh, fill], axis=0).astype(
                jnp.bfloat16
            )

    return pl.pallas_call(
        kernel,
        out_shape=(
            jax.ShapeDtypeStruct((RD, QR, HD), jnp.bfloat16),
            jax.ShapeDtypeStruct((RD * 16, HD), jnp.bfloat16),
        ),
        in_specs=[pl.BlockSpec(memory_space=SMEM), pl.BlockSpec(memory_space=VMEM)],
        out_specs=[pl.BlockSpec(memory_space=VMEM)] * 2,
        compiler_params=pltpu.CompilerParams(vmem_limit_bytes=LIMIT),
        cost_estimate=pl.CostEstimate(flops=0, bytes_accessed=1 << 20, transcendentals=0),
        name="pick_rows",
    )(info, received)


def attend(info, queries, fresh, pieces):
    n_pieces = len(pieces)

    def kernel(info_ref, qs, fresh_ref, *refs):
        piece_refs = refs[:n_pieces]
        out_ref, kvbuf, kn, vn = refs[n_pieces:]
        z, core = info_ref[5, 0], info_ref[5, 1]
        step = 1 - 2 * core
        def place(piece, unit, side, src_z, src_core):
            owner = lax.rem(src_z + KVH, KVH) * 2 + src_core
            rows = pl.ds(pl.multiple_of(owner * SPAN, SPAN), SPAN)
            kvbuf[side, rows, :] = piece_refs[piece][unit * SPAN : (unit + 1) * SPAN, :]

        for side in range(2):
            place(0, 7 + side, side, z, core)
            place(1, 7 + side, side, z, 1 - core)
            for dist in range(1, 4):
                for half in range(2):
                    unit = 2 * half + side
                    there = core if half == 0 else 1 - core
                    place(1 + dist, unit, side, z - step * dist, there)
                    far, at = (6, 4 * (dist - 1)) if dist < 3 else (7, 0)
                    place(far, at + unit, side, z + step * dist, 1 - there)
        for half in range(2):
            there = core if half == 0 else 1 - core
            place(5, half, core, z + 4, there)
            place(7, 4 + half, 1 - core, z + 4, 1 - there)
        kvbuf[:, KVH * 2 * SPAN :, :] = jnp.zeros((2, WIN, HD), jnp.bfloat16)
        col = lax.broadcasted_iota(jnp.int32, (QR, WIN), 1)
        ncol = lax.broadcasted_iota(jnp.int32, (QR, 16), 1)
        nrow = lax.rem(lax.broadcasted_iota(jnp.int32, (QR, 16), 0), TOK)
        step_k, step_q = ncol // CH, nrow // CH
        pos_k, pos_q = lax.rem(ncol, CH), lax.rem(nrow, CH)
        need = jnp.where((step_k == step_q) & (pos_k <= pos_q), -1, 100)
        need = jnp.where(step_k < step_q, pos_k, need)
        need = jnp.where(ncol < TOK, need, 100)
        trow = lax.rem(lax.broadcasted_iota(jnp.int32, (QR, HD), 0), TOK)
        tstep, tpos = trow // CH, lax.rem(trow, CH)
        mine, theirs = fresh_ref[...].astype(jnp.float32), piece_refs[7][6 * SPAN :, :].astype(jnp.float32)
        low_half = lax.broadcasted_iota(jnp.int32, (RD * 16, HD), 1) < HD // 2
        low = jnp.where(core == 0, mine, theirs)
        high = jnp.where(core == 0, theirs, mine)
        kn[...] = jnp.where(low_half, low, pltpu.roll(high, HD // 2, 1)).astype(jnp.bfloat16)
        vn[...] = jnp.where(low_half, pltpu.roll(low, HD // 2, 1), high).astype(jnp.bfloat16)

        group = 12

        def some(it, carry):
            js = [it * group + i for i in range(group)]
            scores, values = [], []
            for j in js:
                start, length = info_ref[1, j], info_ref[2, j]
                base = pl.multiple_of((start // 16) * 16, 16)
                off = start - base
                keys = jnp.concatenate([kvbuf[0, pl.ds(base, WIN), :], kn[pl.ds(16 * j, 16), :]], axis=0)
                sc = lax.dot_general(
                    qs[j], keys, (((1,), (1,)), ((), ())), preferred_element_type=jnp.float32
                )
                cached = jnp.where(
                    (col >= off) & (col < off + length), sc[:, :WIN] * SCALE, -1e30
                )
                fresh = jnp.where(need <= info_ref[3, j], sc[:, WIN:] * SCALE, -1e30)
                scores.append((cached, fresh))
            weights = []
            for cached, fresh in scores:
                top = jnp.maximum(
                    jnp.max(cached, axis=1, keepdims=True), jnp.max(fresh, axis=1, keepdims=True)
                )
                wc, wf = jnp.exp(cached - top), jnp.exp(fresh - top)
                total = jnp.sum(wc, axis=1, keepdims=True) + jnp.sum(wf, axis=1, keepdims=True)
                weights.append((jnp.concatenate([wc, wf], axis=1), total))
            for j, (w, total) in zip(js, weights):
                base = pl.multiple_of((info_ref[1, j] // 16) * 16, 16)
                vals = jnp.concatenate([kvbuf[1, pl.ds(base, WIN), :], vn[pl.ds(16 * j, 16), :]], axis=0)
                high = w.astype(jnp.bfloat16)
                low = (w - high.astype(jnp.float32)).astype(jnp.bfloat16)
                dims = (((1,), (0,)), ((), ()))
                acc = lax.dot_general(high, vals, dims, preferred_element_type=jnp.float32)
                acc += lax.dot_general(low, vals, dims, preferred_element_type=jnp.float32)
                limit = jnp.where(tstep == 0, info_ref[3, j], info_ref[4, j])
                out = jnp.where(tpos <= limit, acc / total, 0.0)
                out_ref[info_ref[0, j]] = out.astype(jnp.bfloat16)
            return carry

        lax.fori_loop(0, RD // group, some, 0)

    return pl.pallas_call(
        kernel,
        out_shape=jax.ShapeDtypeStruct((64, QR, HD), jnp.bfloat16),
        in_specs=[
            pl.BlockSpec(memory_space=SMEM),
            pl.BlockSpec(memory_space=VMEM),
            pl.BlockSpec(memory_space=VMEM),
        ]
        + [pl.BlockSpec(memory_space=VMEM)] * n_pieces,
        out_specs=pl.BlockSpec(memory_space=VMEM),
        scratch_shapes=[
            pltpu.VMEM((2, KVH * 2 * SPAN + WIN, HD), jnp.bfloat16),
            pltpu.VMEM((RD * 16, HD), jnp.bfloat16),
            pltpu.VMEM((RD * 16, HD), jnp.bfloat16),
        ],
        compiler_params=pltpu.CompilerParams(vmem_limit_bytes=LIMIT),
        cost_estimate=pl.CostEstimate(
            flops=24 * 40 * 400 * 128 * 6, bytes_accessed=4 << 20, transcendentals=24 * 40 * 400
        ),
        name="attend",
    )(info, queries, fresh, *pieces)


def unpack_rows(pos, received):
    def kernel(pos_ref, in_ref, out_ref, scr):
        for j in range(RD):
            block = in_ref[pos_ref[j]].astype(jnp.float32)
            for s in range(STEPS):
                rows = pl.ds(s * CH * RD + j, CH, stride=RD)
                for h in range(PER):
                    row = h * TOK + s * CH
                    scr[h, rows, :] = block[row : row + CH]
        for s in range(STEPS):
            for c in range(CH):
                row = (s * CH + c) * RD
                heads = [scr[h, row : row + RD, :] for h in range(PER)]
                out_ref[s, c] = jnp.concatenate(heads, axis=1).astype(jnp.bfloat16)

    return pl.pallas_call(
        kernel,
        out_shape=jax.ShapeDtypeStruct((STEPS, CH, RD, PER * HD), jnp.bfloat16),
        in_specs=[pl.BlockSpec(memory_space=SMEM), pl.BlockSpec(memory_space=VMEM)],
        out_specs=pl.BlockSpec(memory_space=VMEM),
        scratch_shapes=[pltpu.VMEM((PER, TOK * RD, HD), jnp.float32)],
        compiler_params=pltpu.CompilerParams(vmem_limit_bytes=LIMIT),
        cost_estimate=pl.CostEstimate(flops=0, bytes_accessed=1 << 20, transcendentals=0),
        name="unpack_rows",
    )(pos, received)


def body(queries, kv_cache, new_kv, lengths, accepted, dest):
    me_dp = lax.axis_index("dp")
    me_ten = lax.axis_index("tensor")
    z, core = me_ten // 2, me_ten % 2
    n_dp = lax.axis_size("dp")

    def along_z(x, k):
        perm = [(t, (t // 2 + (k if t % 2 == 0 else -k)) % KVH * 2 + t % 2) for t in range(16)]
        return lax.ppermute(x, "tensor", perm)

    def sibling(x):
        return lax.ppermute(x, "tensor", [(t, t ^ 1) for t in range(16)])

    keep, give = split_cache(jnp.stack([z, core]).astype(jnp.int32), kv_cache)
    got = sibling(give)
    moved = [along_z(x, k + 1) for k, x in enumerate(join_cores(keep, got))]
    crossed_a = sibling(jnp.concatenate(moved[:2], axis=0))

    group_of = dest // RD
    order = jnp.arange(RD)
    here = (group_of == me_dp).reshape(n_dp, RD)
    before = jnp.sum(here[:, None, :] & (order[None, :] < order[:, None]), axis=2)
    place = (jnp.arange(n_dp)[:, None] * 2 + before).reshape(-1)
    hit = dest[None, :] == (me_dp * RD + order)[:, None]
    recv_pos = jnp.sum(jnp.where(hit, place[None, :], 0), axis=1)
    taken = jnp.sum(jnp.where(hit[None], accepted[:, None, :], 0), axis=2)
    length = lengths[0]
    start = jnp.sum(jnp.where(order[None, :] < order[:, None], length[None, :], 0), axis=1)
    ident = jnp.where(order == 0, z, jnp.where(order == 1, core, 0))
    info = jnp.stack([recv_pos, start, length, taken[0], taken[1], ident]).astype(jnp.int32)

    first = (me_dp * RD).reshape(1).astype(jnp.int32)
    first, _ = lax.optimization_barrier((first, give))
    by_token = jnp.transpose(queries, (0, 2, 1, 3)), jnp.transpose(new_kv, (0, 1, 3, 2, 4))
    packed, send_pos = pack_rows(dest, first, *by_token)
    received = lax.all_to_all(packed, "dp", split_axis=0, concat_axis=0, tiled=True)
    rows, fresh = pick_rows(info, received)
    crossed_b = sibling(jnp.concatenate(moved[2:] + [fresh], axis=0))
    outs = attend(info, rows, fresh, [give, got] + moved + [crossed_a, crossed_b])
    back = lax.all_to_all(
        outs.reshape(n_dp, 2 * QR, HD), "dp", split_axis=0, concat_axis=0, tiled=True
    )
    out = unpack_rows(send_pos, back.reshape(2 * n_dp, QR, HD))
    return jnp.transpose(out, (0, 2, 1, 3))


def solution(mesh):
    return jax.shard_map(
        body,
        mesh=mesh,
        in_specs=(
            P(None, "dp", None, "tensor"),
            P(None, ("dp", "tensor"), None),
            P(None, None, "dp", None, "tensor"),
            P("dp", None),
            P(),
            P(),
        ),
        out_specs=P(None, "dp", None, "tensor"),
        check_vma=False,
    )
```

```python
import jax
import jax.numpy as jnp
from jax import lax
from jax.experimental import pallas as pl
from jax.experimental.pallas import tpu as pltpu
from jax.sharding import PartitionSpec as P

HQ = 64
KVH = 8
HD = 128
CH = 5
STEPS = 2
RD = 24
SPAN = 256
WIN = 384
TOK = STEPS * CH
PER = 4
QR = PER * TOK
PITCH = 56
SCALE = HD**-0.5
VMEM = pltpu.MemorySpace.VMEM
SMEM = pltpu.MemorySpace.SMEM
LIMIT = 48 * 1024 * 1024


def split_cache(ident, kv):
    def kernel(id_ref, kv_ref, keep_ref, give_ref):
        z, core = id_ref[0], id_ref[1]
        step = 1 - 2 * core

        def put(ref, unit, side, dist):
            col = pl.multiple_of(lax.rem(z + dist + KVH, KVH) * HD, HD)
            ref[unit * SPAN : (unit + 1) * SPAN, :] = kv_ref[side, :, pl.ds(col, HD)]

        for dist in range(1, 4):
            for side in range(2):
                put(give_ref, 2 * (dist - 1) + side, side, -dist * step)
                put(keep_ref, 2 * (dist - 1) + side, side, dist * step)
        put(give_ref, 6, 1 - core, 4)
        put(keep_ref, 6, core, 4)
        put(give_ref, 7, 0, 0)
        put(give_ref, 8, 1, 0)

    return pl.pallas_call(
        kernel,
        out_shape=(
            jax.ShapeDtypeStruct((7 * SPAN, HD), kv.dtype),
            jax.ShapeDtypeStruct((9 * SPAN, HD), kv.dtype),
        ),
        in_specs=[pl.BlockSpec(memory_space=SMEM), pl.BlockSpec(memory_space=VMEM)],
        out_specs=[pl.BlockSpec(memory_space=VMEM)] * 2,
        compiler_params=pltpu.CompilerParams(vmem_limit_bytes=LIMIT),
        cost_estimate=pl.CostEstimate(flops=0, bytes_accessed=2 << 20, transcendentals=0),
        name="split_cache",
    )(ident, kv)


def join_cores(keep, got):
    sizes = [4, 4, 4, 2]

    def kernel(keep_ref, got_ref, *outs):
        for i, out in enumerate(outs):
            rows = sizes[i] // 2 * SPAN
            out[:rows, :] = keep_ref[2 * i * SPAN : 2 * i * SPAN + rows, :]
            out[rows:, :] = got_ref[2 * i * SPAN : 2 * i * SPAN + rows, :]

    return pl.pallas_call(
        kernel,
        out_shape=[jax.ShapeDtypeStruct((n * SPAN, HD), keep.dtype) for n in sizes],
        in_specs=[pl.BlockSpec(memory_space=VMEM)] * 2,
        out_specs=[pl.BlockSpec(memory_space=VMEM)] * 4,
        compiler_params=pltpu.CompilerParams(vmem_limit_bytes=LIMIT),
        cost_estimate=pl.CostEstimate(flops=0, bytes_accessed=2 << 20, transcendentals=0),
        name="join_cores",
    )(keep, got)


def pack_rows(dest, first, queries, new_kv):
    def kernel(dest_ref, first_ref, q_ref, n_ref, out_ref, pos_ref, seen, flat, qs, ns):
        for g in range(32):
            seen[g] = 0
        for j in range(RD):
            g = dest_ref[first_ref[0] + j] // RD
            pos_ref[j] = 2 * g + seen[g]
            seen[g] = 1
        for s in range(STEPS):
            for c in range(CH):
                row = s * CH + c
                q = q_ref[s, c].astype(jnp.float32)
                for h in range(PER):
                    rows = pl.ds(h * TOK + row, RD, stride=PITCH)
                    flat[rows, :] = q[:, h * HD : (h + 1) * HD]
                n = [n_ref[side, s, c].astype(jnp.float32) for side in range(2)]
                flat[pl.ds(QR + row, RD, stride=PITCH), :] = jnp.concatenate(n, axis=1)
        for j in range(RD):
            at = pos_ref[j]
            qs[at] = flat[j * PITCH : j * PITCH + QR, :]
            ns[at] = flat[j * PITCH + QR : j * PITCH + QR + TOK, :]
        for g in range(32):
            block = [qs[2 * g], qs[2 * g + 1], ns[2 * g], ns[2 * g + 1]]
            out_ref[g] = jnp.concatenate(block, axis=0).astype(jnp.bfloat16)

    return pl.pallas_call(
        kernel,
        out_shape=(
            jax.ShapeDtypeStruct((32, 2 * (QR + TOK), HD), jnp.bfloat16),
            jax.ShapeDtypeStruct((RD,), jnp.int32),
        ),
        in_specs=[
            pl.BlockSpec(memory_space=SMEM),
            pl.BlockSpec(memory_space=SMEM),
            pl.BlockSpec(memory_space=VMEM),
            pl.BlockSpec(memory_space=VMEM),
        ],
        out_specs=(pl.BlockSpec(memory_space=VMEM), pl.BlockSpec(memory_space=SMEM)),
        scratch_shapes=[
            pltpu.SMEM((32,), jnp.int32),
            pltpu.VMEM((RD * PITCH, HD), jnp.float32),
            pltpu.VMEM((64, QR, HD), jnp.float32),
            pltpu.VMEM((64, TOK, HD), jnp.float32),
        ],
        compiler_params=pltpu.CompilerParams(vmem_limit_bytes=LIMIT),
        cost_estimate=pl.CostEstimate(flops=0, bytes_accessed=2 << 20, transcendentals=0),
        name="pack_rows",
    )(dest, first, queries, new_kv)


def pick_rows(info, received):
    def kernel(info_ref, recv_ref, q_ref, n_ref):
        fill = jnp.zeros((16 - TOK, HD), jnp.float32)
        base = 2 * QR
        for j in range(RD):
            at = info_ref[0, j]
            g, second = at // 2, lax.rem(at, 2) == 1
            block = recv_ref[g].astype(jnp.float32)
            q_ref[j] = jnp.where(second, block[QR : 2 * QR], block[:QR]).astype(jnp.bfloat16)
            fresh = jnp.where(second, block[base + TOK :], block[base : base + TOK])
            n_ref[16 * j : 16 * j + 16, :] = jnp.concatenate([fresh, fill], axis=0).astype(
                jnp.bfloat16
            )

    return pl.pallas_call(
        kernel,
        out_shape=(
            jax.ShapeDtypeStruct((RD, QR, HD), jnp.bfloat16),
            jax.ShapeDtypeStruct((RD * 16, HD), jnp.bfloat16),
        ),
        in_specs=[pl.BlockSpec(memory_space=SMEM), pl.BlockSpec(memory_space=VMEM)],
        out_specs=[pl.BlockSpec(memory_space=VMEM)] * 2,
        compiler_params=pltpu.CompilerParams(vmem_limit_bytes=LIMIT),
        cost_estimate=pl.CostEstimate(flops=0, bytes_accessed=1 << 20, transcendentals=0),
        name="pick_rows",
    )(info, received)


def attend(info, queries, fresh, pieces):
    n_pieces = len(pieces)

    def kernel(info_ref, qs, fresh_ref, *refs):
        piece_refs = refs[:n_pieces]
        out_ref, kvbuf, kn, vn = refs[n_pieces:]
        z, core = info_ref[5, 0], info_ref[5, 1]
        step = 1 - 2 * core
        def place(piece, unit, side, src_z, src_core):
            owner = lax.rem(src_z + KVH, KVH) * 2 + src_core
            rows = pl.ds(pl.multiple_of(owner * SPAN, SPAN), SPAN)
            kvbuf[side, rows, :] = piece_refs[piece][unit * SPAN : (unit + 1) * SPAN, :]

        for side in range(2):
            place(0, 7 + side, side, z, core)
            place(1, 7 + side, side, z, 1 - core)
            for dist in range(1, 4):
                for half in range(2):
                    unit = 2 * half + side
                    there = core if half == 0 else 1 - core
                    place(1 + dist, unit, side, z - step * dist, there)
                    far, at = (6, 4 * (dist - 1)) if dist < 3 else (7, 0)
                    place(far, at + unit, side, z + step * dist, 1 - there)
        for half in range(2):
            there = core if half == 0 else 1 - core
            place(5, half, core, z + 4, there)
            place(7, 4 + half, 1 - core, z + 4, 1 - there)
        kvbuf[:, KVH * 2 * SPAN :, :] = jnp.zeros((2, WIN, HD), jnp.bfloat16)
        col = lax.broadcasted_iota(jnp.int32, (QR, WIN), 1)
        ncol = lax.broadcasted_iota(jnp.int32, (QR, 16), 1)
        nrow = lax.rem(lax.broadcasted_iota(jnp.int32, (QR, 16), 0), TOK)
        step_k, step_q = ncol // CH, nrow // CH
        pos_k, pos_q = lax.rem(ncol, CH), lax.rem(nrow, CH)
        need = jnp.where((step_k == step_q) & (pos_k <= pos_q), -1, 100)
        need = jnp.where(step_k < step_q, pos_k, need)
        need = jnp.where(ncol < TOK, need, 100)
        trow = lax.rem(lax.broadcasted_iota(jnp.int32, (QR, HD), 0), TOK)
        tstep, tpos = trow // CH, lax.rem(trow, CH)
        mine, theirs = fresh_ref[...].astype(jnp.float32), piece_refs[7][6 * SPAN :, :].astype(jnp.float32)
        low_half = lax.broadcasted_iota(jnp.int32, (RD * 16, HD), 1) < HD // 2
        low = jnp.where(core == 0, mine, theirs)
        high = jnp.where(core == 0, theirs, mine)
        kn[...] = jnp.where(low_half, low, pltpu.roll(high, HD // 2, 1)).astype(jnp.bfloat16)
        vn[...] = jnp.where(low_half, pltpu.roll(low, HD // 2, 1), high).astype(jnp.bfloat16)

        scores, weights = [], []
        for j in range(RD):
            start, length = info_ref[1, j], info_ref[2, j]
            base = pl.multiple_of((start // 16) * 16, 16)
            off = start - base
            keys = jnp.concatenate([kvbuf[0, pl.ds(base, WIN), :], kn[pl.ds(16 * j, 16), :]], axis=0)
            sc = lax.dot_general(
                qs[j], keys, (((1,), (1,)), ((), ())), preferred_element_type=jnp.float32
            )
            cached = jnp.where(
                (col >= off) & (col < off + length), sc[:, :WIN] * SCALE, -1e30
            )
            fresh = jnp.where(need <= info_ref[3, j], sc[:, WIN:] * SCALE, -1e30)
            scores.append((cached, fresh))
        for cached, fresh in scores:
            top = jnp.maximum(
                jnp.max(cached, axis=1, keepdims=True), jnp.max(fresh, axis=1, keepdims=True)
            )
            wc, wf = jnp.exp(cached - top), jnp.exp(fresh - top)
            total = jnp.sum(wc, axis=1, keepdims=True) + jnp.sum(wf, axis=1, keepdims=True)
            weights.append((jnp.concatenate([wc, wf], axis=1), total))
        for j, (w, total) in enumerate(weights):
            base = pl.multiple_of((info_ref[1, j] // 16) * 16, 16)
            vals = jnp.concatenate([kvbuf[1, pl.ds(base, WIN), :], vn[pl.ds(16 * j, 16), :]], axis=0)
            high = w.astype(jnp.bfloat16)
            low = (w - high.astype(jnp.float32)).astype(jnp.bfloat16)
            dims = (((1,), (0,)), ((), ()))
            both = jnp.concatenate([high, low], axis=0)
            both = lax.dot_general(both, vals, dims, preferred_element_type=jnp.float32)
            acc = both[:QR] + both[QR:]
            limit = jnp.where(tstep == 0, info_ref[3, j], info_ref[4, j])
            out = jnp.where(tpos <= limit, acc / total, 0.0)
            out_ref[info_ref[0, j]] = out.astype(jnp.bfloat16)

    return pl.pallas_call(
        kernel,
        out_shape=jax.ShapeDtypeStruct((64, QR, HD), jnp.bfloat16),
        in_specs=[
            pl.BlockSpec(memory_space=SMEM),
            pl.BlockSpec(memory_space=VMEM),
            pl.BlockSpec(memory_space=VMEM),
        ]
        + [pl.BlockSpec(memory_space=VMEM)] * n_pieces,
        out_specs=pl.BlockSpec(memory_space=VMEM),
        scratch_shapes=[
            pltpu.VMEM((2, KVH * 2 * SPAN + WIN, HD), jnp.bfloat16),
            pltpu.VMEM((RD * 16, HD), jnp.bfloat16),
            pltpu.VMEM((RD * 16, HD), jnp.bfloat16),
        ],
        compiler_params=pltpu.CompilerParams(vmem_limit_bytes=LIMIT),
        cost_estimate=pl.CostEstimate(
            flops=24 * 40 * 400 * 128 * 6, bytes_accessed=4 << 20, transcendentals=24 * 40 * 400
        ),
        name="attend",
    )(info, queries, fresh, *pieces)


def unpack_rows(pos, received):
    def kernel(pos_ref, in_ref, out_ref, scr):
        for j in range(RD):
            scr[j * QR : (j + 1) * QR, :] = in_ref[pos_ref[j]].astype(jnp.float32)
        for s in range(STEPS):
            for c in range(CH):
                at = s * CH + c
                heads = [scr[pl.ds(h * TOK + at, RD, stride=QR), :] for h in range(PER)]
                out_ref[s, c] = jnp.concatenate(heads, axis=1).astype(jnp.bfloat16)

    return pl.pallas_call(
        kernel,
        out_shape=jax.ShapeDtypeStruct((STEPS, CH, RD, PER * HD), jnp.bfloat16),
        in_specs=[pl.BlockSpec(memory_space=SMEM), pl.BlockSpec(memory_space=VMEM)],
        out_specs=pl.BlockSpec(memory_space=VMEM),
        scratch_shapes=[pltpu.VMEM((RD * QR, HD), jnp.float32)],
        compiler_params=pltpu.CompilerParams(vmem_limit_bytes=LIMIT),
        cost_estimate=pl.CostEstimate(flops=0, bytes_accessed=1 << 20, transcendentals=0),
        name="unpack_rows",
    )(pos, received)


def body(queries, kv_cache, new_kv, lengths, accepted, dest):
    me_dp = lax.axis_index("dp")
    me_ten = lax.axis_index("tensor")
    z, core = me_ten // 2, me_ten % 2
    n_dp = lax.axis_size("dp")

    def along_z(x, k):
        perm = [(t, (t // 2 + (k if t % 2 == 0 else -k)) % KVH * 2 + t % 2) for t in range(16)]
        return lax.ppermute(x, "tensor", perm)

    def sibling(x):
        return lax.ppermute(x, "tensor", [(t, t ^ 1) for t in range(16)])

    keep, give = split_cache(jnp.stack([z, core]).astype(jnp.int32), kv_cache)
    got = sibling(give)
    moved = [along_z(x, k + 1) for k, x in enumerate(join_cores(keep, got))]
    crossed_a = sibling(jnp.concatenate(moved[:2], axis=0))

    group_of = dest // RD
    order = jnp.arange(RD)
    here = (group_of == me_dp).reshape(n_dp, RD)
    before = jnp.sum(here[:, None, :] & (order[None, :] < order[:, None]), axis=2)
    place = (jnp.arange(n_dp)[:, None] * 2 + before).reshape(-1)
    hit = dest[None, :] == (me_dp * RD + order)[:, None]
    recv_pos = jnp.sum(jnp.where(hit, place[None, :], 0), axis=1)
    taken = jnp.sum(jnp.where(hit[None], accepted[:, None, :], 0), axis=2)
    length = lengths[0]
    start = jnp.sum(jnp.where(order[None, :] < order[:, None], length[None, :], 0), axis=1)
    ident = jnp.where(order == 0, z, jnp.where(order == 1, core, 0))
    info = jnp.stack([recv_pos, start, length, taken[0], taken[1], ident]).astype(jnp.int32)

    first = (me_dp * RD).reshape(1).astype(jnp.int32)
    first, _ = lax.optimization_barrier((first, give))
    by_token = jnp.transpose(queries, (0, 2, 1, 3)), jnp.transpose(new_kv, (0, 1, 3, 2, 4))
    packed, send_pos = pack_rows(dest, first, *by_token)
    received = lax.all_to_all(packed, "dp", split_axis=0, concat_axis=0, tiled=True)
    rows, fresh = pick_rows(info, received)
    crossed_b = sibling(jnp.concatenate(moved[2:] + [fresh], axis=0))
    outs = attend(info, rows, fresh, [give, got] + moved + [crossed_a, crossed_b])
    back = lax.all_to_all(
        outs.reshape(n_dp, 2 * QR, HD), "dp", split_axis=0, concat_axis=0, tiled=True
    )
    out = unpack_rows(send_pos, back.reshape(2 * n_dp, QR, HD))
    return jnp.transpose(out, (0, 2, 1, 3))


def solution(mesh):
    return jax.shard_map(
        body,
        mesh=mesh,
        in_specs=(
            P(None, "dp", None, "tensor"),
            P(None, ("dp", "tensor"), None),
            P(None, None, "dp", None, "tensor"),
            P("dp", None),
            P(),
            P(),
        ),
        out_specs=P(None, "dp", None, "tensor"),
        check_vma=False,
    )
```

```python
import jax
import jax.numpy as jnp
from jax import lax
from jax.experimental import pallas as pl
from jax.experimental.pallas import tpu as pltpu
from jax.sharding import PartitionSpec as P

HQ = 64
KVH = 8
HD = 128
CH = 5
STEPS = 2
RD = 24
SPAN = 256
WIN = 384
TOK = STEPS * CH
PER = 4
QR = PER * TOK
PITCH = 56
SCALE = HD**-0.5
VMEM = pltpu.MemorySpace.VMEM
SMEM = pltpu.MemorySpace.SMEM
LIMIT = 48 * 1024 * 1024


def split_cache(ident, kv):
    def kernel(id_ref, kv_ref, keep_ref, give_ref):
        z, core = id_ref[0], id_ref[1]
        step = 1 - 2 * core

        def put(ref, unit, side, dist):
            col = pl.multiple_of(lax.rem(z + dist + KVH, KVH) * HD, HD)
            ref[unit * SPAN : (unit + 1) * SPAN, :] = kv_ref[side, :, pl.ds(col, HD)]

        for dist in range(1, 4):
            for side in range(2):
                put(give_ref, 2 * (dist - 1) + side, side, -dist * step)
                put(keep_ref, 2 * (dist - 1) + side, side, dist * step)
        put(give_ref, 6, 1 - core, 4)
        put(keep_ref, 6, core, 4)
        put(give_ref, 7, 0, 0)
        put(give_ref, 8, 1, 0)

    return pl.pallas_call(
        kernel,
        out_shape=(
            jax.ShapeDtypeStruct((7 * SPAN, HD), kv.dtype),
            jax.ShapeDtypeStruct((9 * SPAN, HD), kv.dtype),
        ),
        in_specs=[pl.BlockSpec(memory_space=SMEM), pl.BlockSpec(memory_space=VMEM)],
        out_specs=[pl.BlockSpec(memory_space=VMEM)] * 2,
        compiler_params=pltpu.CompilerParams(vmem_limit_bytes=LIMIT),
        cost_estimate=pl.CostEstimate(flops=0, bytes_accessed=2 << 20, transcendentals=0),
        name="split_cache",
    )(ident, kv)


def join_cores(keep, got):
    sizes = [4, 4, 4, 2]

    def kernel(keep_ref, got_ref, *outs):
        for i, out in enumerate(outs):
            rows = sizes[i] // 2 * SPAN
            out[:rows, :] = keep_ref[2 * i * SPAN : 2 * i * SPAN + rows, :]
            out[rows:, :] = got_ref[2 * i * SPAN : 2 * i * SPAN + rows, :]

    return pl.pallas_call(
        kernel,
        out_shape=[jax.ShapeDtypeStruct((n * SPAN, HD), keep.dtype) for n in sizes],
        in_specs=[pl.BlockSpec(memory_space=VMEM)] * 2,
        out_specs=[pl.BlockSpec(memory_space=VMEM)] * 4,
        compiler_params=pltpu.CompilerParams(vmem_limit_bytes=LIMIT),
        cost_estimate=pl.CostEstimate(flops=0, bytes_accessed=2 << 20, transcendentals=0),
        name="join_cores",
    )(keep, got)


def pack_rows(dest, first, queries, new_kv):
    def kernel(dest_ref, first_ref, q_ref, n_ref, out_ref, pos_ref, seen, flat, qs, ns):
        for g in range(32):
            seen[g] = 0
        for j in range(RD):
            g = dest_ref[first_ref[0] + j] // RD
            pos_ref[j] = 2 * g + seen[g]
            seen[g] = 1
        for s in range(STEPS):
            for c in range(CH):
                row = s * CH + c
                q = q_ref[s, c].astype(jnp.float32)
                for h in range(PER):
                    rows = pl.ds(h * TOK + row, RD, stride=PITCH)
                    flat[rows, :] = q[:, h * HD : (h + 1) * HD]
                n = [n_ref[side, s, c].astype(jnp.float32) for side in range(2)]
                flat[pl.ds(QR + row, RD, stride=PITCH), :] = jnp.concatenate(n, axis=1)
        for j in range(RD):
            at = pos_ref[j]
            qs[at] = flat[j * PITCH : j * PITCH + QR, :]
            ns[at] = flat[j * PITCH + QR : j * PITCH + QR + TOK, :]
        for g in range(32):
            block = [qs[2 * g], qs[2 * g + 1], ns[2 * g], ns[2 * g + 1]]
            out_ref[g] = jnp.concatenate(block, axis=0).astype(jnp.bfloat16)

    return pl.pallas_call(
        kernel,
        out_shape=(
            jax.ShapeDtypeStruct((32, 2 * (QR + TOK), HD), jnp.bfloat16),
            jax.ShapeDtypeStruct((RD,), jnp.int32),
        ),
        in_specs=[
            pl.BlockSpec(memory_space=SMEM),
            pl.BlockSpec(memory_space=SMEM),
            pl.BlockSpec(memory_space=VMEM),
            pl.BlockSpec(memory_space=VMEM),
        ],
        out_specs=(pl.BlockSpec(memory_space=VMEM), pl.BlockSpec(memory_space=SMEM)),
        scratch_shapes=[
            pltpu.SMEM((32,), jnp.int32),
            pltpu.VMEM((RD * PITCH, HD), jnp.float32),
            pltpu.VMEM((64, QR, HD), jnp.float32),
            pltpu.VMEM((64, TOK, HD), jnp.float32),
        ],
        compiler_params=pltpu.CompilerParams(vmem_limit_bytes=LIMIT),
        cost_estimate=pl.CostEstimate(flops=0, bytes_accessed=2 << 20, transcendentals=0),
        name="pack_rows",
    )(dest, first, queries, new_kv)


def pick_rows(info, received):
    def kernel(info_ref, recv_ref, q_ref, n_ref):
        fill = jnp.zeros((16 - TOK, HD), jnp.float32)
        base = 2 * QR
        for j in range(RD):
            at = info_ref[0, j]
            g, second = at // 2, lax.rem(at, 2) == 1
            block = recv_ref[g].astype(jnp.float32)
            q_ref[j] = jnp.where(second, block[QR : 2 * QR], block[:QR]).astype(jnp.bfloat16)
            fresh = jnp.where(second, block[base + TOK :], block[base : base + TOK])
            n_ref[16 * j : 16 * j + 16, :] = jnp.concatenate([fresh, fill], axis=0).astype(
                jnp.bfloat16
            )

    return pl.pallas_call(
        kernel,
        out_shape=(
            jax.ShapeDtypeStruct((RD, QR, HD), jnp.bfloat16),
            jax.ShapeDtypeStruct((RD * 16, HD), jnp.bfloat16),
        ),
        in_specs=[pl.BlockSpec(memory_space=SMEM), pl.BlockSpec(memory_space=VMEM)],
        out_specs=[pl.BlockSpec(memory_space=VMEM)] * 2,
        compiler_params=pltpu.CompilerParams(vmem_limit_bytes=LIMIT),
        cost_estimate=pl.CostEstimate(flops=0, bytes_accessed=1 << 20, transcendentals=0),
        name="pick_rows",
    )(info, received)


def attend(info, queries, fresh, pieces):
    n_pieces = len(pieces)

    def kernel(info_ref, qs, fresh_ref, *refs):
        piece_refs = refs[:n_pieces]
        out_ref, kvbuf, kn, vn = refs[n_pieces:]
        z, core = info_ref[5, 0], info_ref[5, 1]
        step = 1 - 2 * core
        def place(piece, unit, side, src_z, src_core):
            owner = lax.rem(src_z + KVH, KVH) * 2 + src_core
            rows = pl.ds(pl.multiple_of(owner * SPAN, SPAN), SPAN)
            kvbuf[side, rows, :] = piece_refs[piece][unit * SPAN : (unit + 1) * SPAN, :]

        for side in range(2):
            place(0, 7 + side, side, z, core)
            place(1, 7 + side, side, z, 1 - core)
            for dist in range(1, 4):
                for half in range(2):
                    unit = 2 * half + side
                    there = core if half == 0 else 1 - core
                    place(1 + dist, unit, side, z - step * dist, there)
                    far, at = (7, 0) if dist == 2 else (6, 2 * (dist - 1))
                    place(far, at + unit, side, z + step * dist, 1 - there)
        for half in range(2):
            there = core if half == 0 else 1 - core
            place(5, half, core, z + 4, there)
            place(7, 4 + half, 1 - core, z + 4, 1 - there)
        kvbuf[:, KVH * 2 * SPAN :, :] = jnp.zeros((2, WIN, HD), jnp.bfloat16)
        col = lax.broadcasted_iota(jnp.int32, (QR, WIN), 1)
        ncol = lax.broadcasted_iota(jnp.int32, (QR, 16), 1)
        nrow = lax.rem(lax.broadcasted_iota(jnp.int32, (QR, 16), 0), TOK)
        step_k, step_q = ncol // CH, nrow // CH
        pos_k, pos_q = lax.rem(ncol, CH), lax.rem(nrow, CH)
        need = jnp.where((step_k == step_q) & (pos_k <= pos_q), -1, 100)
        need = jnp.where(step_k < step_q, pos_k, need)
        need = jnp.where(ncol < TOK, need, 100)
        trow = lax.rem(lax.broadcasted_iota(jnp.int32, (QR, HD), 0), TOK)
        tstep, tpos = trow // CH, lax.rem(trow, CH)
        mine, theirs = fresh_ref[...].astype(jnp.float32), piece_refs[7][6 * SPAN :, :].astype(jnp.float32)
        low_half = lax.broadcasted_iota(jnp.int32, (RD * 16, HD), 1) < HD // 2
        low = jnp.where(core == 0, mine, theirs)
        high = jnp.where(core == 0, theirs, mine)
        kn[...] = jnp.where(low_half, low, pltpu.roll(high, HD // 2, 1)).astype(jnp.bfloat16)
        vn[...] = jnp.where(low_half, pltpu.roll(low, HD // 2, 1), high).astype(jnp.bfloat16)

        scores, weights = [], []
        for j in range(RD):
            start, length = info_ref[1, j], info_ref[2, j]
            base = pl.multiple_of((start // 16) * 16, 16)
            off = start - base
            keys = jnp.concatenate([kvbuf[0, pl.ds(base, WIN), :], kn[pl.ds(16 * j, 16), :]], axis=0)
            sc = lax.dot_general(
                qs[j], keys, (((1,), (1,)), ((), ())), preferred_element_type=jnp.float32
            )
            cached = jnp.where(
                (col >= off) & (col < off + length), sc[:, :WIN] * SCALE, -1e30
            )
            fresh = jnp.where(need <= info_ref[3, j], sc[:, WIN:] * SCALE, -1e30)
            scores.append((cached, fresh))
        for cached, fresh in scores:
            top = jnp.maximum(
                jnp.max(cached, axis=1, keepdims=True), jnp.max(fresh, axis=1, keepdims=True)
            )
            wc, wf = jnp.exp(cached - top), jnp.exp(fresh - top)
            total = jnp.sum(wc, axis=1, keepdims=True) + jnp.sum(wf, axis=1, keepdims=True)
            weights.append((jnp.concatenate([wc, wf], axis=1), total))
        for j, (w, total) in enumerate(weights):
            base = pl.multiple_of((info_ref[1, j] // 16) * 16, 16)
            vals = jnp.concatenate([kvbuf[1, pl.ds(base, WIN), :], vn[pl.ds(16 * j, 16), :]], axis=0)
            high = w.astype(jnp.bfloat16)
            low = (w - high.astype(jnp.float32)).astype(jnp.bfloat16)
            dims = (((1,), (0,)), ((), ()))
            both = jnp.concatenate([high, low], axis=0)
            both = lax.dot_general(both, vals, dims, preferred_element_type=jnp.float32)
            acc = both[:QR] + both[QR:]
            limit = jnp.where(tstep == 0, info_ref[3, j], info_ref[4, j])
            out = jnp.where(tpos <= limit, acc / total, 0.0)
            out_ref[info_ref[0, j]] = out.astype(jnp.bfloat16)

    return pl.pallas_call(
        kernel,
        out_shape=jax.ShapeDtypeStruct((64, QR, HD), jnp.bfloat16),
        in_specs=[
            pl.BlockSpec(memory_space=SMEM),
            pl.BlockSpec(memory_space=VMEM),
            pl.BlockSpec(memory_space=VMEM),
        ]
        + [pl.BlockSpec(memory_space=VMEM)] * n_pieces,
        out_specs=pl.BlockSpec(memory_space=VMEM),
        scratch_shapes=[
            pltpu.VMEM((2, KVH * 2 * SPAN + WIN, HD), jnp.bfloat16),
            pltpu.VMEM((RD * 16, HD), jnp.bfloat16),
            pltpu.VMEM((RD * 16, HD), jnp.bfloat16),
        ],
        compiler_params=pltpu.CompilerParams(vmem_limit_bytes=LIMIT),
        cost_estimate=pl.CostEstimate(
            flops=24 * 40 * 400 * 128 * 6, bytes_accessed=4 << 20, transcendentals=24 * 40 * 400
        ),
        name="attend",
    )(info, queries, fresh, *pieces)


def unpack_rows(pos, received):
    def kernel(pos_ref, in_ref, out_ref, scr):
        for j in range(RD):
            scr[j * QR : (j + 1) * QR, :] = in_ref[pos_ref[j]].astype(jnp.float32)
        for s in range(STEPS):
            for c in range(CH):
                at = s * CH + c
                heads = [scr[pl.ds(h * TOK + at, RD, stride=QR), :] for h in range(PER)]
                out_ref[s, c] = jnp.concatenate(heads, axis=1).astype(jnp.bfloat16)

    return pl.pallas_call(
        kernel,
        out_shape=jax.ShapeDtypeStruct((STEPS, CH, RD, PER * HD), jnp.bfloat16),
        in_specs=[pl.BlockSpec(memory_space=SMEM), pl.BlockSpec(memory_space=VMEM)],
        out_specs=pl.BlockSpec(memory_space=VMEM),
        scratch_shapes=[pltpu.VMEM((RD * QR, HD), jnp.float32)],
        compiler_params=pltpu.CompilerParams(vmem_limit_bytes=LIMIT),
        cost_estimate=pl.CostEstimate(flops=0, bytes_accessed=1 << 20, transcendentals=0),
        name="unpack_rows",
    )(pos, received)


def body(queries, kv_cache, new_kv, lengths, accepted, dest):
    me_dp = lax.axis_index("dp")
    me_ten = lax.axis_index("tensor")
    z, core = me_ten // 2, me_ten % 2
    n_dp = lax.axis_size("dp")

    def along_z(x, k):
        perm = [(t, (t // 2 + (k if t % 2 == 0 else -k)) % KVH * 2 + t % 2) for t in range(16)]
        return lax.ppermute(x, "tensor", perm)

    def sibling(x):
        return lax.ppermute(x, "tensor", [(t, t ^ 1) for t in range(16)])

    keep, give = split_cache(jnp.stack([z, core]).astype(jnp.int32), kv_cache)
    got = sibling(give)
    moved = [along_z(x, k + 1) for k, x in enumerate(join_cores(keep, got))]
    crossed_a = sibling(jnp.concatenate([moved[0], moved[2]], axis=0))

    order = jnp.arange(RD)
    index = jnp.arange(dest.shape[0])
    hit = dest[None, :] == (me_dp * RD + order)[:, None]
    row = jnp.sum(jnp.where(hit, index[None, :], 0), axis=1)
    source = row // RD
    here = (dest >= me_dp * RD) & (dest < (me_dp + 1) * RD)
    before = here[None, :] & (index[None, :] // RD == source[:, None]) & (index[None, :] < row[:, None])
    recv_pos = source * 2 + jnp.sum(before, axis=1)
    taken = jnp.sum(jnp.where(hit[None], accepted[:, None, :], 0), axis=2)
    length = lengths[0]
    start = jnp.sum(jnp.where(order[None, :] < order[:, None], length[None, :], 0), axis=1)
    ident = jnp.where(order == 0, z, jnp.where(order == 1, core, 0))
    info = jnp.stack([recv_pos, start, length, taken[0], taken[1], ident]).astype(jnp.int32)

    first = (me_dp * RD).reshape(1).astype(jnp.int32)
    first, _ = lax.optimization_barrier((first, give))
    by_token = jnp.transpose(queries, (0, 2, 1, 3)), jnp.transpose(new_kv, (0, 1, 3, 2, 4))
    packed, send_pos = pack_rows(dest, first, *by_token)
    received = lax.all_to_all(packed, "dp", split_axis=0, concat_axis=0, tiled=True)
    rows, fresh = pick_rows(info, received)
    crossed_b = sibling(jnp.concatenate([moved[1], moved[3], fresh], axis=0))
    outs = attend(info, rows, fresh, [give, got] + moved + [crossed_a, crossed_b])
    back = lax.all_to_all(
        outs.reshape(n_dp, 2 * QR, HD), "dp", split_axis=0, concat_axis=0, tiled=True
    )
    out = unpack_rows(send_pos, back.reshape(2 * n_dp, QR, HD))
    return jnp.transpose(out, (0, 2, 1, 3))


def solution(mesh):
    return jax.shard_map(
        body,
        mesh=mesh,
        in_specs=(
            P(None, "dp", None, "tensor"),
            P(None, ("dp", "tensor"), None),
            P(None, None, "dp", None, "tensor"),
            P("dp", None),
            P(),
            P(),
        ),
        out_specs=P(None, "dp", None, "tensor"),
        check_vma=False,
    )
```
